32 devices in a mesh: grp: 2 (over y), seq: 4 (over z), head: 4 (over x, core).
Axes of the slice: x: 2, y: 2, z: 4, core: 2. Of those that a mesh axis runs over, the one named last changes fastest.
Arguments:
- q_heads: bfloat16 [8, 64, 16384], P('head', None, ('grp', 'seq')), parts along dimension 2, may hold values from -12 to 12
- k_heads: bfloat16 [8, 64, 16384], P('head', None, ('grp', 'seq')), parts along dimension 2, may hold values from -10 to 10
- v_heads: bfloat16 [8, 64, 16384], P('head', None, ('grp', 'seq')), parts along dimension 2, may hold values from -10 to 10
- morton_order: int32 [8, 2048], P(('grp', 'seq')), parts along dimension 0, may hold values from 0 to 2047, each once within a row
- leaf_counts: int32 [64], P('grp'), parts along dimension 0, may hold values from 64 to 256, as said below
Outputs:
- attended: bfloat16 [8, 64, 16384], P('head', None, ('grp', 'seq')), parts along dimension 2
The draws below stay inside these ranges and needn't reach their ends.
There are 2 independent parts, one for each index of `grp`. The reference program is written for one: setup_inputs(seed, part) draws one part's arguments, and reference() takes and returns one part's arrays. A program takes and returns all parts, laid end to end along the dimension named above; each array names one. Nothing has to cross between parts.
Inputs may be any that keep to these rules, and one draw needn't show every extreme that they name: `morton_order`: each row holds every number of 0 .. 2047 once. `leaf_counts`: the valid points of a leaf are its first ones.
All inputs are finite; a program needn't handle non-finite values.
Results may differ from the reference program's by a relative error of at most 0.0021.
Values may be sent and summed in bfloat16 or wider, within the bound.
A program may use at most 64 MiB of HBM per device.

```python
import math
import jax
import jax.numpy as jnp
from jax import lax

HEADS = 8
HEAD_SIZE = 64
LEAF_POINTS = 256
TOK_DEV = 2048
TOKENS = 8192
BLOCKS = 4


def multiscale(key):
    leaves = TOKENS // LEAF_POINTS
    scale_count = leaves.bit_length()
    field = jnp.zeros((HEADS, HEAD_SIZE, TOKENS), jnp.float32)
    for level_index in range(scale_count):
        pieces = max(leaves >> level_index, 1)
        coarse = jax.random.normal(jax.random.fold_in(key, 100 + level_index), (HEADS, HEAD_SIZE, pieces), jnp.float32)
        field = field + jnp.repeat(coarse, TOKENS // pieces, axis=2)
    return field / math.sqrt(scale_count)


def draw_q_heads(key, part):
    shape = (HEADS, HEAD_SIZE, TOKENS)
    smooth = multiscale(jax.random.fold_in(key, 15))
    rough = jax.random.normal(jax.random.fold_in(key, 13), shape, jnp.float32)
    values = 1.4 * rough + 0.9 * smooth
    return jnp.clip(values, -12.0, 12.0).astype(jnp.bfloat16)


def draw_k_heads(key, part):
    shape = (HEADS, HEAD_SIZE, TOKENS)
    smooth = multiscale(jax.random.fold_in(key, 16))
    rough = jax.random.normal(jax.random.fold_in(key, 12), shape, jnp.float32)
    values = 1.4 * rough + 0.9 * smooth
    return jnp.clip(values, -10.0, 10.0).astype(jnp.bfloat16)


def draw_v_heads(key, part):
    shape = (HEADS, HEAD_SIZE, TOKENS)
    smooth = multiscale(jax.random.fold_in(key, 32))
    rough = jax.random.normal(jax.random.fold_in(key, 31), shape, jnp.float32)
    values = 1.5 * rough + 1.5 * smooth
    return jnp.clip(values, -10.0, 10.0).astype(jnp.bfloat16)


def draw_leaf_counts(key, part):
    raw_counts = jax.random.randint(jax.random.fold_in(key, 41), (TOKENS // LEAF_POINTS,), LEAF_POINTS // 4, 2 * LEAF_POINTS, jnp.int32)
    return jnp.minimum(raw_counts, LEAF_POINTS).astype(jnp.int32)


def setup_inputs(seed: int = 0, part: int = 0) -> dict:
    streams_of = jax.random.split(jax.random.key(seed), 6)
    own_keys = jax.random.split(jax.random.fold_in(streams_of[5], part), 6)
    return {
        "q_heads": draw_q_heads(jax.random.fold_in(jax.random.fold_in(streams_of[5], part), 71), part),
        "k_heads": draw_k_heads(jax.random.fold_in(jax.random.fold_in(streams_of[5], part), 71), part),
        "v_heads": draw_v_heads(jax.random.fold_in(jax.random.fold_in(streams_of[5], part), 71), part),
        "morton_order": jax.vmap(lambda own: jax.random.permutation(own, TOK_DEV))(jax.random.split(own_keys[3], BLOCKS)).reshape((BLOCKS, TOK_DEV)).astype(jnp.int32),
        "leaf_counts": draw_leaf_counts(jax.random.fold_in(jax.random.fold_in(streams_of[5], part), 71), part),
    }


NEG_FILL = -1e+30

def valid_points(leaf_counts):
    slots = jnp.arange(LEAF_POINTS, dtype=jnp.int32)
    return (slots[None, :] < leaf_counts[:, None]).astype(jnp.float32).reshape(-1)

def pooled(values, group_len):
    new_shape = values.shape[:-1] + (values.shape[-1] // group_len, group_len)
    return lax.optimization_barrier(jnp.sum(values.reshape(new_shape), axis=-1, dtype=jnp.float32))

def sibling_rows(values, block_rows):
    new_shape = values.shape[:-1] + (values.shape[-1] // (2 * block_rows), 2, block_rows)
    return jnp.flip(values.reshape(new_shape), axis=-2).reshape(values.shape)

def near_field(query_rows, key_rows, value_rows, valid):
    leaves = TOKENS // LEAF_POINTS
    scale_multiplier = 1.0 / math.sqrt(HEAD_SIZE)
    key_pad = jnp.pad(key_rows, ((0, 0), (LEAF_POINTS, LEAF_POINTS))).reshape(HEAD_SIZE, leaves + 2, LEAF_POINTS)
    value_pad = jnp.pad(value_rows, ((0, 0), (LEAF_POINTS, LEAF_POINTS))).reshape(HEAD_SIZE, leaves + 2, LEAF_POINTS)
    valid_pad = jnp.pad(valid, (LEAF_POINTS, LEAF_POINTS)).reshape(leaves + 2, LEAF_POINTS)
    key_win = jnp.concatenate([key_pad[:, offset:offset + leaves] for offset in range(3)], axis=-1)
    value_win = jnp.concatenate([value_pad[:, offset:offset + leaves] for offset in range(3)], axis=-1)
    valid_win = jnp.concatenate([valid_pad[offset:offset + leaves] for offset in range(3)], axis=-1)
    group = math.gcd(leaves, 64)
    batches = leaves // group
    query_grp = jnp.moveaxis(query_rows.reshape(HEAD_SIZE, batches, group, LEAF_POINTS), 1, 0)
    key_grp = jnp.moveaxis(key_win.reshape(HEAD_SIZE, batches, group, 3 * LEAF_POINTS), 1, 0)
    value_grp = jnp.moveaxis(value_win.reshape(HEAD_SIZE, batches, group, 3 * LEAF_POINTS), 1, 0)
    valid_grp = valid_win.reshape(batches, group, 3 * LEAF_POINTS)

    def one_batch(pieces):
        query_piece, key_piece, value_piece, mask_piece = pieces
        logit_scores = jnp.einsum('dnq,dnk->nqk', query_piece.astype(jnp.float32), key_piece.astype(jnp.float32)) * scale_multiplier
        logit_scores = jnp.where(mask_piece[:, None, :] > 0, logit_scores, NEG_FILL)
        best_score = lax.optimization_barrier(jnp.max(logit_scores, axis=-1))
        weight_probs = jnp.exp(logit_scores - best_score[..., None])
        weight_sum = lax.optimization_barrier(jnp.sum(weight_probs, axis=-1))
        probabilities = weight_probs.astype(jnp.bfloat16)
        blended_sum = jnp.einsum('nqk,dnk->dnq', probabilities.astype(jnp.float32), value_piece.astype(jnp.float32))
        return (best_score, blended_sum, weight_sum)
    best_all, mixed_all, total_all = lax.map(one_batch, (query_grp, key_grp, value_grp, valid_grp))
    mixed_all = jnp.moveaxis(mixed_all, 0, 1).reshape(HEAD_SIZE, TOKENS)
    return (best_all.reshape(-1), mixed_all, total_all.reshape(-1))

def far_field(query_rows, key_rows, value_rows, valid, level_index):
    group_len = 2 ** level_index
    scale_multiplier = 1.0 / math.sqrt(HEAD_SIZE)
    mean_query = pooled(query_rows.astype(jnp.float32), group_len) / group_len
    key_sums = pooled(key_rows.astype(jnp.float32) * valid, group_len)
    value_sums = pooled(value_rows.astype(jnp.float32) * valid, group_len)
    masses = pooled(valid, group_len)
    block_groups = TOKENS // (group_len * LEAF_POINTS)
    far_mass = sibling_rows(masses, LEAF_POINTS)
    mean_keys = sibling_rows(key_sums, LEAF_POINTS) / jnp.maximum(far_mass, 1.0)
    distant_values = sibling_rows(value_sums, LEAF_POINTS)
    mass_rows = far_mass.reshape(block_groups, LEAF_POINTS)
    logit_scores = jnp.einsum('swj,swg->wjg', mean_query.reshape(HEAD_SIZE, block_groups, LEAF_POINTS), mean_keys.reshape(HEAD_SIZE, block_groups, LEAF_POINTS), precision=lax.Precision.HIGHEST) * scale_multiplier
    logit_scores = jnp.where(mass_rows[:, None, :] > 0, logit_scores, NEG_FILL)
    best_score = lax.optimization_barrier(jnp.max(logit_scores, axis=-1))
    weight_probs = jnp.exp(logit_scores - best_score[..., None])
    weight_sum = lax.optimization_barrier(jnp.sum(weight_probs * mass_rows[:, None, :], axis=-1))
    blended_sum = jnp.einsum('rto,pro->prt', weight_probs, distant_values.reshape(HEAD_SIZE, block_groups, LEAF_POINTS), precision=lax.Precision.HIGHEST)
    return (best_score.reshape(-1), blended_sum.reshape(HEAD_SIZE, -1), weight_sum.reshape(-1))

def reference(q_heads, k_heads, v_heads, morton_order, leaf_counts):
    offsets = (jnp.arange(morton_order.shape[0], dtype=jnp.int32) * TOK_DEV)[:, None]
    gather_index = (morton_order + offsets).reshape(-1).astype(jnp.int32)
    query_all = jnp.take(q_heads, gather_index, axis=2)
    key_all = jnp.take(k_heads, gather_index, axis=2)
    value_all = jnp.take(v_heads, gather_index, axis=2)
    valid = valid_points(leaf_counts)
    depth_all = (TOKENS // LEAF_POINTS).bit_length() - 1

    def one_head(pieces):
        query_rows, key_rows, value_rows = pieces
        near_best, near_mixed, near_total = near_field(query_rows, key_rows, value_rows, valid)
        far_terms = []
        for level_index in range(1, depth_all):
            far_terms.append((2 ** level_index, far_field(query_rows, key_rows, value_rows, valid, level_index)))
        best_score = near_best
        for group_len, term in far_terms:
            best_score = jnp.maximum(best_score, jnp.repeat(term[0], group_len))
        factor = jnp.exp(near_best - best_score)
        blended_sum = near_mixed * factor[None, :]
        weight_sum = near_total * factor
        for group_len, term in far_terms:
            factor = jnp.exp(jnp.repeat(term[0], group_len) - best_score)
            blended_sum = blended_sum + jnp.repeat(term[1], group_len, axis=-1) * factor[None, :]
            weight_sum = weight_sum + jnp.repeat(term[2], group_len) * factor
        return (blended_sum / weight_sum[None, :]).astype(jnp.bfloat16)
    return lax.map(one_head, (query_all, key_all, value_all))
```

```python
import functools
import math

import jax
import jax.numpy as jnp
from jax import lax
from jax.experimental import pallas as pl
from jax.experimental.pallas import tpu as pltpu
from jax.sharding import PartitionSpec as P

LEAF = 256
NEG = -1e30
BF = jnp.bfloat16
F32 = jnp.float32
PAD = 16


def dot(a, b, dims=((1,), (0,))):
    return lax.dot_general(a, b, (dims, ((), ())), preferred_element_type=F32)


def split(x):
    hi = x.astype(BF)
    return hi, (x - hi.astype(F32)).astype(BF)


def kernel(cfg, *refs):
    heads, width, tokens, seq_count = cfg
    rows = heads * width
    leaves = tokens // LEAF
    depth_local = leaves.bit_length() - 1
    depth_all = (leaves * seq_count).bit_length() - 1
    levels = list(range(1, depth_all))
    far_levels = [l for l in levels if l >= depth_local]
    scale = math.log2(math.e) / math.sqrt(width)
    refs = list(refs)
    take = lambda n: [refs.pop(0) for _ in range(n)]
    q_hbm, k_hbm, v_hbm, order, counts, out = take(6)
    xin, xp, kva, ktx, vx, num, stat = take(7)
    us = dict(zip(levels, take(len(levels))))
    fs = dict(zip(levels, take(len(levels))))
    qs = dict(zip(far_levels, take(len(far_levels))))
    kmp = dict(zip(far_levels, take(len(far_levels))))
    vvp = dict(zip(far_levels, take(len(far_levels))))
    kmr = dict(zip(far_levels, take(len(far_levels))))
    vvr = dict(zip(far_levels, take(len(far_levels))))
    in_sem, halo_send, halo_recv = take(3)
    far_send = dict(zip(far_levels, take(len(far_levels))))
    far_recv = dict(zip(far_levels, take(len(far_levels))))

    seq = lax.axis_index("seq")
    has_left, has_right = seq > 0, seq < seq_count - 1

    loads = [
        pltpu.make_async_copy(src, xin.at[pl.ds(i * rows, rows)], in_sem.at[i])
        for i, src in enumerate((q_hbm, k_hbm, v_hbm))
    ]
    for load in loads:
        load.start()
    barrier = pltpu.get_barrier_semaphore()
    for step in range(1, seq_count):
        other = lax.rem(seq + step, seq_count)
        pl.semaphore_signal(
            barrier, inc=1, device_id={"seq": other}, device_id_type=pl.DeviceIdType.MESH
        )

    @pl.when(jnp.logical_not(has_left))
    def _():
        ktx[0:LEAF, :] = jnp.zeros((LEAF, rows), BF)
        vx[:, 0:LEAF] = jnp.zeros((rows, LEAF), BF)

    @pl.when(jnp.logical_not(has_right))
    def _():
        ktx[tokens + LEAF :, :] = jnp.zeros((LEAF, rows), BF)
        vx[:, tokens + LEAF :] = jnp.zeros((rows, LEAF), BF)

    def count_of(n):
        leaf = seq * leaves + n
        total = leaves * seq_count
        inside = jnp.logical_and(leaf >= 0, leaf < total)
        return jnp.where(inside, counts[jnp.clip(leaf, 0, total - 1)], 0)

    def build(level):
        u = us[level]
        r = lax.broadcasted_iota(jnp.int32, u.shape, 0)
        t = lax.broadcasted_iota(jnp.int32, u.shape, 1)
        u[...] = jnp.where((t >> level) == r, 1.0, 0.0).astype(BF)

    for level in levels:
        build(level)
    for load in loads:
        load.wait()

    def permute(n):
        at = n * LEAF
        if not isinstance(n, int):
            at = pl.multiple_of(at, LEAF)
        picks = order[0:1, pl.ds(at, LEAF)]
        spots = lax.broadcasted_iota(jnp.int32, (tokens, LEAF), 0)
        hot = jnp.where(spots == picks, 1.0, 0.0).astype(BF)
        moved = dot(xin[...], hot)
        count = count_of(n)
        query, key, value = moved[:rows], moved[rows : 2 * rows], moved[2 * rows :]
        key_t = key.T
        on_row = lax.broadcasted_iota(jnp.int32, (rows, LEAF), 1) < count
        on_col = lax.broadcasted_iota(jnp.int32, (LEAF, rows), 0) < count
        xp[0:rows, pl.ds(at, LEAF)] = query.astype(BF)
        xp[rows : 2 * rows, pl.ds(at, LEAF)] = jnp.where(on_row, value, 0.0).astype(BF)
        xp[2 * rows :, pl.ds(at, LEAF)] = jnp.where(on_row[:PAD], 1.0, 0.0).astype(BF)
        kva[pl.ds(at, LEAF), 0:rows] = jnp.where(on_col, key_t, 0.0).astype(BF)
        kva[pl.ds(at, LEAF), rows:] = jnp.where(on_col, 1.0, 0.0).astype(BF)
        ktx[pl.ds(at + LEAF, LEAF), :] = key_t.astype(BF)
        vx[:, pl.ds(at + LEAF, LEAF)] = value.astype(BF)

    permute(0)
    permute(leaves - 1)
    pl.semaphore_wait(barrier, seq_count - 1)

    def remote(src, dst, send, recv, target):
        return pltpu.make_async_remote_copy(
            src_ref=src,
            dst_ref=dst,
            send_sem=send,
            recv_sem=recv,
            device_id={"seq": target},
            device_id_type=pl.DeviceIdType.MESH,
        )

    def halo(side):
        start, end = (LEAF, tokens + LEAF) if side == 0 else (tokens, 0)
        target = jnp.maximum(seq - 1, 0) if side == 0 else jnp.minimum(seq + 1, seq_count - 1)
        return (
            remote(
                ktx.at[pl.ds(start, LEAF)],
                ktx.at[pl.ds(end, LEAF)],
                halo_send.at[2 * side],
                halo_recv.at[2 * side],
                target,
            ),
            remote(
                vx.at[:, pl.ds(start, LEAF)],
                vx.at[:, pl.ds(end, LEAF)],
                halo_send.at[2 * side + 1],
                halo_recv.at[2 * side + 1],
                target,
            ),
        )

    @pl.when(has_left)
    def _():
        for copy in halo(0):
            copy.start()

    @pl.when(has_right)
    def _():
        for copy in halo(1):
            copy.start()

    if leaves > 2:

        @pl.loop(1, leaves - 1)
        def _(n):
            permute(n)

    def pool(level, off, span):
        u = us[level][...]
        kk = dot(u, kva[pl.ds(off, span), :])
        mass = kk[:, rows:]
        km_hi, km_lo = split(kk[:, :rows] / jnp.maximum(mass, 1.0))
        xx = dot(xp[:, pl.ds(off, span)], u, ((1,), (1,)))
        q_hi, q_lo = split(xx[:rows] * (1.0 / 2**level))
        v_hi, v_lo = split(xx[rows : 2 * rows])
        km = jnp.concatenate([km_hi, km_lo], axis=1)
        vv = jnp.concatenate([v_hi, v_lo, xx[2 * rows :].astype(BF)], axis=0)
        return (q_hi, q_lo), km, vv, mass

    def far(query, km, vvs, bias, store):
        q_hi, q_lo = query
        count = q_hi.shape[1]
        for h in range(heads):
            keep = lax.broadcasted_iota(jnp.int32, (rows, count), 0) // width == h
            zero = jnp.zeros((rows, count), F32)
            hi = jnp.where(keep, q_hi.astype(F32), zero).astype(BF)
            lo = jnp.where(keep, q_lo.astype(F32), zero).astype(BF)
            s = dot(km, jnp.concatenate([hi, hi], axis=0)) + dot(km[:, :rows], lo)
            if count <= 128:
                s = s + bias[:, :count]
            else:
                s = s + jnp.concatenate([bias[:, :128]] * (count // 128), axis=1)
            best = jnp.max(s, axis=0, keepdims=True).astype(BF)
            w_hi, w_lo = split(jnp.exp2((s - best.astype(F32)) * scale))
            step = 0
            acc = jnp.zeros((width + PAD, count), F32)
            for vv in vvs:
                keys = vv.shape[1]
                v_hi = vv[h * width : (h + 1) * width]
                v_lo = vv[rows + h * width : rows + (h + 1) * width]
                mass = vv[2 * rows :]
                left = jnp.concatenate([v_hi, mass], axis=0)
                acc = acc + dot(left, w_hi[step : step + keys])
                acc = acc + dot(left, w_lo[step : step + keys])
                low = dot(v_lo, w_hi[step : step + keys])
                acc = acc + jnp.concatenate([low, jnp.zeros((PAD, count), F32)], axis=0)
                step += keys
            a_hi, a_lo = split(acc)
            tops = jnp.broadcast_to(best.astype(F32), (PAD, count)).astype(BF)
            store(h, jnp.concatenate([a_hi, a_lo, tops], axis=0))

    def far_copies(level):
        bit = level - depth_local
        nb = 1 << bit
        part = tokens >> level
        slot = lax.rem(seq, nb)
        base = ((seq >> bit) ^ 1) << bit
        copies = []
        for j in range(nb):
            target = base + j
            copies.append(
                remote(
                    kmp[level],
                    kmr[level].at[pl.ds(pl.multiple_of(slot * part, part), part)],
                    far_send[level].at[2 * j],
                    far_recv[level].at[2 * slot],
                    target,
                )
            )
            copies.append(
                remote(
                    vvp[level],
                    vvr[level].at[slot],
                    far_send[level].at[2 * j + 1],
                    far_recv[level].at[2 * slot + 1],
                    target,
                )
            )
        return copies

    for level in reversed(far_levels):
        (q_hi, q_lo), km, vv, _ = pool(level, 0, tokens)
        qs[level][0:rows, :] = q_hi
        qs[level][rows:, :] = q_lo
        kmp[level][...] = km
        vvp[level][...] = vv
        for copy in far_copies(level):
            copy.start()

    for level in levels:
        if level in far_levels:
            continue
        span = LEAF << level
        for pair in range(tokens // span // 2):
            sides = [pool(level, (2 * pair + i) * span, span) for i in range(2)]
            for i in range(2):
                query = sides[i][0]
                _, km, vv, mass = sides[1 - i]
                bias = jnp.where(mass > 0, 0.0, NEG)
                first = (2 * pair + i) * LEAF

                def store(h, value):
                    fs[level][h, :, first : first + LEAF] = value

                far(query, km, [vv], bias, store)

    def near(n):
        at = n * LEAF
        if not isinstance(n, int):
            at = pl.multiple_of(at, LEAF)
        window = ktx[pl.ds(at, 3 * LEAF), :]
        query = xp[0:rows, pl.ds(at, LEAF)].astype(F32)
        spots = lax.broadcasted_iota(jnp.int32, (LEAF, LEAF), 0)
        for h in range(heads):
            keep = lax.broadcasted_iota(jnp.int32, (rows, LEAF), 0) // width == h
            s = dot(window, jnp.where(keep, query, 0.0).astype(BF))
            s = jnp.concatenate(
                [
                    jnp.where(spots < count_of(n - 1 + i), s[i * LEAF : (i + 1) * LEAF], NEG)
                    for i in range(3)
                ],
                axis=0,
            )
            best = jnp.max(s, axis=0, keepdims=True)
            w = jnp.exp2((s - best) * scale)
            total = jnp.sum(w, axis=0, keepdims=True)
            value = vx[h * width : (h + 1) * width, pl.ds(at, 3 * LEAF)]
            num[h * width : (h + 1) * width, pl.ds(at, LEAF)] = dot(value, w.astype(BF))
            stat[2 * h : 2 * h + 1, pl.ds(at, LEAF)] = best
            stat[2 * h + 1 : 2 * h + 2, pl.ds(at, LEAF)] = total

    if leaves > 2:

        @pl.loop(1, leaves - 1)
        def _(n):
            near(n)

    @pl.when(has_right)
    def _():
        for copy in halo(0):
            copy.wait_recv()

    @pl.when(has_left)
    def _():
        for copy in halo(1):
            copy.wait_recv()

    near(0)
    near(leaves - 1)

    for level in far_levels:
        nb = 1 << (level - depth_local)
        part = tokens >> level
        for i in range(nb):
            remote(
                kmp[level], kmr[level].at[pl.ds(i * part, part)],
                far_send[level].at[2 * i], far_recv[level].at[2 * i], seq,
            ).wait_recv()
            remote(
                vvp[level], vvr[level].at[i],
                far_send[level].at[2 * i + 1], far_recv[level].at[2 * i + 1], seq,
            ).wait_recv()
        query = (qs[level][0:rows, :], qs[level][rows:, :])
        vvs = [vvr[level][i] for i in range(nb)]
        ones = jnp.ones((PAD, 128), BF)
        mass = jnp.concatenate(
            [dot(vv[2 * rows :], ones, ((0,), (0,))) for vv in vvs], axis=0
        )
        bias = jnp.where(mass > 0, 0.0, NEG)

        def store(h, value):
            fs[level][h] = value

        far(query, kmr[level][...], vvs, bias, store)

    def finish(n):
        at = pl.multiple_of(n * LEAF, LEAF)
        for h in range(heads):
            near_best = stat[2 * h : 2 * h + 1, pl.ds(at, LEAF)]
            near_total = stat[2 * h + 1 : 2 * h + 2, pl.ds(at, LEAF)]
            blocks = []
            best = near_best
            size = width + PAD
            for level in levels:
                if level in far_levels:
                    f = fs[level][h]
                    u = us[level][:, pl.ds(at, LEAF)]
                else:
                    g = 1 << level
                    f = fs[level][h, :, pl.ds(pl.multiple_of((n >> level) * LEAF, LEAF), LEAF)]
                    u = us[level][:, pl.ds(pl.multiple_of((n & (g - 1)) * LEAF, LEAF), LEAF)]
                up = dot(f, u)
                top = up[2 * size : 2 * size + 1]
                blocks.append((up[:size] + up[size : 2 * size], top))
                best = jnp.maximum(best, top)
            factor = jnp.exp2((near_best - best) * scale)
            top = num[h * width : (h + 1) * width, pl.ds(at, LEAF)] * factor
            bottom = near_total * factor
            for block, level_best in blocks:
                factor = jnp.exp2((level_best - best) * scale)
                top = top + block[:width] * factor
                bottom = bottom + block[width : width + 1] * factor
            out[h * width : (h + 1) * width, pl.ds(at, LEAF)] = (top / bottom).astype(BF)

    @pl.loop(0, leaves)
    def _(n):
        finish(n)

    @pl.when(has_left)
    def _():
        for copy in halo(0):
            copy.wait_send()

    @pl.when(has_right)
    def _():
        for copy in halo(1):
            copy.wait_send()

    for level in far_levels:
        for copy in far_copies(level):
            copy.wait_send()


def shards(q_heads, k_heads, v_heads, morton_order, leaf_counts):
    heads_real, width, tokens = q_heads.shape
    heads = heads_real + heads_real % 2
    seq_count = lax.axis_size("seq")
    rows = heads * width
    flat = []
    for x in (q_heads, k_heads, v_heads):
        if heads != heads_real:
            x = jnp.concatenate([x, jnp.zeros_like(x[:1])], axis=0)
        flat.append(x.reshape(rows, tokens))
    leaves = tokens // LEAF
    depth_local = leaves.bit_length() - 1
    depth_all = (leaves * seq_count).bit_length() - 1
    levels = list(range(1, depth_all))
    far_levels = [l for l in levels if l >= depth_local]
    coarse = lambda l: min(LEAF, tokens >> l)
    vm = pltpu.VMEM
    scratch = [
        vm((3 * rows, tokens), BF),
        vm((2 * rows + PAD, tokens), BF),
        vm((tokens, 2 * rows), BF),
        vm((tokens + 2 * LEAF, rows), BF),
        vm((rows, tokens + 2 * LEAF), BF),
        vm((rows, tokens), F32),
        vm((2 * heads + (-2 * heads) % 8, tokens), F32),
    ]
    scratch += [vm((coarse(l), min(LEAF << l, tokens)), BF) for l in levels]
    scratch += [vm((heads, 2 * (width + PAD) + PAD, tokens >> l), BF) for l in levels]
    scratch += [vm((2 * rows, tokens >> l), BF) for l in far_levels]
    scratch += [vm((tokens >> l, 2 * rows), BF) for l in far_levels]
    scratch += [vm((2 * rows + PAD, tokens >> l), BF) for l in far_levels]
    scratch += [vm((LEAF, 2 * rows), BF) for l in far_levels]
    scratch += [
        vm((1 << (l - depth_local), 2 * rows + PAD, tokens >> l), BF) for l in far_levels
    ]
    sem = pltpu.SemaphoreType.DMA
    scratch += [sem((3,)), sem((4,)), sem((4,))]
    scratch += [sem((2 << (l - depth_local),)) for l in far_levels] * 2
    out = pl.pallas_call(
        functools.partial(kernel, (heads, width, tokens, seq_count)),
        out_shape=jax.ShapeDtypeStruct((rows, tokens), BF),
        in_specs=[pl.BlockSpec(memory_space=pl.ANY)] * 3
        + [
            pl.BlockSpec(memory_space=pltpu.VMEM),
            pl.BlockSpec(memory_space=pltpu.SMEM),
        ],
        out_specs=pl.BlockSpec(memory_space=pltpu.VMEM),
        scratch_shapes=scratch,
        compiler_params=pltpu.CompilerParams(
            collective_id=0, has_side_effects=True, vmem_limit_bytes=48 * 1024 * 1024
        ),
    )(*flat, morton_order, leaf_counts)
    return out.reshape(heads, width, tokens)[:heads_real]


def solution(mesh):
    placed = (
        P("head", None, ("grp", "seq")),
        P("head", None, ("grp", "seq")),
        P("head", None, ("grp", "seq")),
        P(("grp", "seq"), None),
        P("grp"),
    )
    return jax.shard_map(
        shards,
        mesh=mesh,
        in_specs=placed,
        out_specs=P("head", None, ("grp", "seq")),
        check_vma=False,
    )
```

```python
import functools
import math

import jax
import jax.numpy as jnp
from jax import lax
from jax.experimental import pallas as pl
from jax.experimental.pallas import tpu as pltpu
from jax.sharding import PartitionSpec as P

LEAF = 256
NEG = -1e30
BF = jnp.bfloat16
F32 = jnp.float32
PAD = 16
BOUND = 10.0
STEPS = 32700.0
VMEM_LIMIT = 63 * 1024 * 1024 + 512 * 1024


def dot(a, b, dims=((1,), (0,))):
    return lax.dot_general(a, b, (dims, ((), ())), preferred_element_type=F32)


def split(x):
    hi = x.astype(BF)
    return hi, (x - hi.astype(F32)).astype(BF)


def kernel(cfg, *refs):
    heads, width, tokens, seq_count = cfg
    rows = heads * width
    leaves = tokens // LEAF
    depth_local = leaves.bit_length() - 1
    depth_all = (leaves * seq_count).bit_length() - 1
    levels = list(range(1, depth_all))
    far_levels = [l for l in levels if l >= depth_local]
    scale = math.log2(math.e) / math.sqrt(width)
    refs = list(refs)
    take = lambda n: [refs.pop(0) for _ in range(n)]
    q_hbm, k_hbm, v_hbm, order_hbm, counts_hbm, out = take(6)
    order, counts = take(2)
    xin, xp, kva, ktx, vx, num, stat = take(7)
    us = dict(zip(levels, take(len(levels))))
    qb, kmb, vvb, biasb, fb = take(5)
    fs = dict(zip(far_levels, take(len(far_levels))))
    qs = dict(zip(far_levels, take(len(far_levels))))
    kmp = dict(zip(far_levels, take(len(far_levels))))
    vvp = dict(zip(far_levels, take(len(far_levels))))
    kmr = dict(zip(far_levels, take(len(far_levels))))
    vvr = dict(zip(far_levels, take(len(far_levels))))
    in_sem, halo_send, halo_recv = take(3)
    far_send = dict(zip(far_levels, take(len(far_levels))))
    far_recv = dict(zip(far_levels, take(len(far_levels))))

    seq = lax.axis_index("seq")
    has_left, has_right = seq > 0, seq < seq_count - 1

    loads = [
        pltpu.make_async_copy(src, xin.at[pl.ds(i * rows, rows)], in_sem.at[i])
        for i, src in enumerate((q_hbm, k_hbm, v_hbm))
    ]
    loads.append(pltpu.make_async_copy(order_hbm, order, in_sem.at[3]))
    loads.append(pltpu.make_async_copy(counts_hbm, counts, in_sem.at[4]))
    for load in loads:
        load.start()
    barrier = pltpu.get_barrier_semaphore()
    for step in range(1, seq_count):
        other = lax.rem(seq + step, seq_count)
        pl.semaphore_signal(
            barrier, inc=1, device_id={"seq": other}, device_id_type=pl.DeviceIdType.MESH
        )

    @pl.when(jnp.logical_not(has_left))
    def _():
        ktx[0:LEAF, :] = jnp.zeros((LEAF, rows), BF)
        vx[:, 0:LEAF] = jnp.zeros((rows, LEAF), BF)

    @pl.when(jnp.logical_not(has_right))
    def _():
        ktx[tokens + LEAF :, :] = jnp.zeros((LEAF, rows), BF)
        vx[:, tokens + LEAF :] = jnp.zeros((rows, LEAF), BF)

    def count_of(n):
        leaf = seq * leaves + n
        total = leaves * seq_count
        inside = jnp.logical_and(leaf >= 0, leaf < total)
        return jnp.where(inside, counts[jnp.clip(leaf, 0, total - 1)], 0)

    def build(level):
        u = us[level]
        r = lax.broadcasted_iota(jnp.int32, u.shape, 0)
        t = lax.broadcasted_iota(jnp.int32, u.shape, 1)
        u[...] = jnp.where((t >> level) == r, 1.0, 0.0).astype(BF)

    for level in levels:
        build(level)
    for load in loads:
        load.wait()

    def permute(n):
        at = n * LEAF
        if not isinstance(n, int):
            at = pl.multiple_of(at, LEAF)
        picks = order[0:1, pl.ds(at, LEAF)]
        spots = lax.broadcasted_iota(jnp.int32, (tokens, LEAF), 0)
        hot = jnp.where(spots == picks, 1.0, 0.0).astype(BF)
        moved = dot(xin[...], hot)
        count = count_of(n)
        query, key, value = moved[:rows], moved[rows : 2 * rows], moved[2 * rows :]
        key_t = key.T
        on_row = lax.broadcasted_iota(jnp.int32, (rows, LEAF), 1) < count
        on_col = lax.broadcasted_iota(jnp.int32, (LEAF, rows), 0) < count
        xp[0:rows, pl.ds(at, LEAF)] = query.astype(BF)
        xp[rows : 2 * rows, pl.ds(at, LEAF)] = jnp.where(on_row, value, 0.0).astype(BF)
        xp[2 * rows :, pl.ds(at, LEAF)] = jnp.where(on_row[:PAD], 1.0, 0.0).astype(BF)
        kva[pl.ds(at, LEAF), 0:rows] = jnp.where(on_col, key_t, 0.0).astype(BF)
        kva[pl.ds(at, LEAF), rows:] = jnp.where(on_col, 1.0, 0.0).astype(BF)
        ktx[pl.ds(at + LEAF, LEAF), :] = key_t.astype(BF)
        vx[:, pl.ds(at + LEAF, LEAF)] = value.astype(BF)

    def remote(src, dst, send, recv, target):
        return pltpu.make_async_remote_copy(
            src_ref=src,
            dst_ref=dst,
            send_sem=send,
            recv_sem=recv,
            device_id={"seq": target},
            device_id_type=pl.DeviceIdType.MESH,
        )

    def halo(side):
        start, end = (LEAF, tokens + LEAF) if side == 0 else (tokens, 0)
        target = jnp.maximum(seq - 1, 0) if side == 0 else jnp.minimum(seq + 1, seq_count - 1)
        return (
            remote(
                ktx.at[pl.ds(start, LEAF)],
                ktx.at[pl.ds(end, LEAF)],
                halo_send.at[2 * side],
                halo_recv.at[2 * side],
                target,
            ),
            remote(
                vx.at[:, pl.ds(start, LEAF)],
                vx.at[:, pl.ds(end, LEAF)],
                halo_send.at[2 * side + 1],
                halo_recv.at[2 * side + 1],
                target,
            ),
        )

    @pl.loop(0, leaves)
    def _(i):
        n = jnp.where(i == 0, 0, jnp.where(i == 1, leaves - 1, i - 1))
        permute(n)

        @pl.when(i == 1)
        def _():
            pl.semaphore_wait(barrier, seq_count - 1)

        @pl.when(jnp.logical_and(i == 1, has_left))
        def _():
            for copy in halo(0):
                copy.start()

        @pl.when(jnp.logical_and(i == 1, has_right))
        def _():
            for copy in halo(1):
                copy.start()

    def pool(level, off, span):
        u = us[level][...]
        kk = dot(u, kva[pl.ds(off, span), :])
        mass = kk[:, rows:]
        mean = kk[:, :rows] / jnp.maximum(mass, 1.0)
        xx = dot(xp[:, pl.ds(off, span)], u, ((1,), (1,)))
        q_hi, q_lo = split(xx[:rows] * (1.0 / 2**level))
        return (q_hi, q_lo), mean, xx[rows : 2 * rows], xx[2 * rows :], mass

    def pack(mean, sums, masses):
        v_hi, v_lo = split(sums)
        km = jnp.concatenate(split(mean), axis=1)
        return km, jnp.concatenate([v_hi, v_lo, masses.astype(BF)], axis=0)

    def fixed(x, bound):
        return jnp.floor(x * (STEPS / bound) + 0.5).astype(jnp.int32).astype(jnp.int16)

    def unfixed(x, bound):
        return x.astype(jnp.int32).astype(F32) * (bound / STEPS)

    def only(x, head):
        blank = jnp.zeros((width, x.shape[1]), x.dtype)
        return jnp.concatenate(
            [x[h * width : (h + 1) * width] if h == head else blank for h in range(heads)],
            axis=0,
        )

    def far(query, km, vvs, bias, store):
        q_hi, q_lo = query
        count = q_hi.shape[1]
        for h in range(heads):
            hi, lo = only(q_hi, h), only(q_lo, h)
            s = dot(km, jnp.concatenate([hi, hi], axis=0)) + dot(km[:, :rows], lo)
            if count <= 128:
                s = s + bias[:, :count]
            else:
                s = s + jnp.concatenate([bias[:, :128]] * (count // 128), axis=1)
            best = jnp.max(s, axis=0, keepdims=True).astype(BF)
            w_hi, w_lo = split(jnp.exp2((s - best.astype(F32)) * scale))
            step = 0
            acc = jnp.zeros((width + PAD, count), F32)
            for vv in vvs:
                keys = vv.shape[1]
                v_hi = vv[h * width : (h + 1) * width]
                v_lo = vv[rows + h * width : rows + (h + 1) * width]
                mass = vv[2 * rows :]
                left = jnp.concatenate([v_hi, mass], axis=0)
                both = dot(jnp.concatenate([left, v_lo], axis=0), w_hi[step : step + keys])
                low = jnp.concatenate([both[width + PAD :], jnp.zeros((PAD, count), F32)], axis=0)
                acc = acc + both[: width + PAD] + low + dot(left, w_lo[step : step + keys])
                step += keys
            a_hi, a_lo = split(acc)
            tops = jnp.broadcast_to(best.astype(F32), (PAD, count)).astype(BF)
            store(h, jnp.concatenate([a_hi, a_lo, tops], axis=0))

    def far_copies(level):
        bit = level - depth_local
        nb = 1 << bit
        part = tokens >> level
        slot = lax.rem(seq, nb)
        base = ((seq >> bit) ^ 1) << bit
        copies = []
        for j in range(nb):
            target = base + j
            copies.append(
                remote(
                    kmp[level],
                    kmr[level].at[pl.ds(pl.multiple_of(slot * part, part), part)],
                    far_send[level].at[2 * j],
                    far_recv[level].at[2 * slot],
                    target,
                )
            )
            copies.append(
                remote(
                    vvp[level],
                    vvr[level].at[slot],
                    far_send[level].at[2 * j + 1],
                    far_recv[level].at[2 * slot + 1],
                    target,
                )
            )
        return copies

    for level in reversed(far_levels):
        (q_hi, q_lo), mean, sums, masses, _ = pool(level, 0, tokens)
        qs[level][0:rows, :] = q_hi
        qs[level][rows:, :] = q_lo
        kmp[level][...] = fixed(mean, BOUND)
        vvp[level][0:rows, :] = fixed(sums, BOUND * 2**level)
        vvp[level][rows:, :] = masses.astype(jnp.int32).astype(jnp.int16)
        for copy in far_copies(level):
            copy.start()

    first = 0
    for level in levels:
        if level in far_levels:
            continue
        span = LEAF << level
        blocks = tokens // span
        start = first

        @pl.loop(0, blocks)
        def _(i):
            (q_hi, q_lo), mean, sums, masses, mass = pool(
                level, pl.multiple_of(i * span, span), span
            )
            km, vv = pack(mean, sums, masses)
            qb[start + i, 0:rows, :] = q_hi
            qb[start + i, rows:, :] = q_lo
            kmb[start + i] = km
            vvb[start + i] = vv
            biasb[start + i] = jnp.where(mass > 0, 0.0, NEG)

        first += blocks

    @pl.loop(0, first, unroll=2)
    def _(i):
        query = (qb[i, 0:rows, :], qb[i, rows:, :])
        other = i + 1 - 2 * lax.rem(i, 2)

        def store(h, value):
            fb[i, h] = value

        far(query, kmb[other], [vvb[other]], biasb[other], store)

    def near(n):
        at = n * LEAF
        if not isinstance(n, int):
            at = pl.multiple_of(at, LEAF)
        window = ktx[pl.ds(at, 3 * LEAF), :]
        query = xp[0:rows, pl.ds(at, LEAF)]
        spots = lax.broadcasted_iota(jnp.int32, (LEAF, LEAF), 0)
        for h in range(heads):
            s = dot(window, only(query, h))
            s = jnp.concatenate(
                [
                    jnp.where(spots < count_of(n - 1 + i), s[i * LEAF : (i + 1) * LEAF], NEG)
                    for i in range(3)
                ],
                axis=0,
            )
            best = jnp.max(s, axis=0, keepdims=True)
            w = jnp.exp2((s - best) * scale)
            total = jnp.sum(w, axis=0, keepdims=True)
            value = vx[h * width : (h + 1) * width, pl.ds(at, 3 * LEAF)]
            num[h * width : (h + 1) * width, pl.ds(at, LEAF)] = dot(value, w.astype(BF))
            stat[2 * h : 2 * h + 1, pl.ds(at, LEAF)] = best
            stat[2 * h + 1 : 2 * h + 2, pl.ds(at, LEAF)] = total

    if leaves > 2:

        @pl.loop(1, leaves - 1, unroll=2)
        def _(n):
            near(n)

    @pl.when(has_right)
    def _():
        for copy in halo(0):
            copy.wait_recv()

    @pl.when(has_left)
    def _():
        for copy in halo(1):
            copy.wait_recv()

    @pl.loop(0, 2, unroll=2)
    def _(i):
        near(i * (leaves - 1))

    for level in far_levels:
        nb = 1 << (level - depth_local)
        part = tokens >> level
        for i in range(nb):
            remote(
                kmp[level], kmr[level].at[pl.ds(i * part, part)],
                far_send[level].at[2 * i], far_recv[level].at[2 * i], seq,
            ).wait_recv()
            remote(
                vvp[level], vvr[level].at[i],
                far_send[level].at[2 * i + 1], far_recv[level].at[2 * i + 1], seq,
            ).wait_recv()
        query = (qs[level][0:rows, :], qs[level][rows:, :])
        means = unfixed(kmr[level][...], BOUND)
        vvs = []
        for i in range(nb):
            sums = unfixed(vvr[level][i, 0:rows], BOUND * 2**level)
            masses = vvr[level][i, rows:].astype(jnp.int32).astype(F32)
            km, vv = pack(means, sums, masses)
            vvs.append(vv)
        ones = jnp.ones((PAD, 128), BF)
        mass = jnp.concatenate(
            [dot(vv[2 * rows :], ones, ((0,), (0,))) for vv in vvs], axis=0
        )
        bias = jnp.where(mass > 0, 0.0, NEG)

        def store(h, value):
            fs[level][h] = value

        far(query, km, vvs, bias, store)

    base_of, first = {}, 0
    for level in levels:
        base_of[level] = first
        first += tokens // (LEAF << level)

    def finish(n):
        at = pl.multiple_of(n * LEAF, LEAF)
        for h in range(heads):
            near_best = stat[2 * h : 2 * h + 1, pl.ds(at, LEAF)]
            near_total = stat[2 * h + 1 : 2 * h + 2, pl.ds(at, LEAF)]
            blocks = []
            best = near_best
            size = width + PAD
            for level in levels:
                if level in far_levels:
                    f = fs[level][h]
                    u = us[level][:, pl.ds(at, LEAF)]
                else:
                    g = 1 << level
                    f = fb[base_of[level] + (n >> level), h]
                    u = us[level][:, pl.ds(pl.multiple_of((n & (g - 1)) * LEAF, LEAF), LEAF)]
                up = dot(f, u)
                top = up[2 * size : 2 * size + 1]
                blocks.append((up[:size] + up[size : 2 * size], top))
                best = jnp.maximum(best, top)
            factor = jnp.exp2((near_best - best) * scale)
            top = num[h * width : (h + 1) * width, pl.ds(at, LEAF)] * factor
            bottom = near_total * factor
            for block, level_best in blocks:
                factor = jnp.exp2((level_best - best) * scale)
                top = top + block[:width] * factor
                bottom = bottom + block[width : width + 1] * factor
            out[h * width : (h + 1) * width, pl.ds(at, LEAF)] = (top * (1.0 / bottom)).astype(BF)

    @pl.loop(0, leaves, unroll=2)
    def _(n):
        finish(n)

    @pl.when(has_left)
    def _():
        for copy in halo(0):
            copy.wait_send()

    @pl.when(has_right)
    def _():
        for copy in halo(1):
            copy.wait_send()

    for level in far_levels:
        for copy in far_copies(level):
            copy.wait_send()


def shards(q_heads, k_heads, v_heads, morton_order, leaf_counts):
    heads_real, width, tokens = q_heads.shape
    heads = heads_real + heads_real % 2
    seq_count = lax.axis_size("seq")
    rows = heads * width
    flat = []
    for x in (q_heads, k_heads, v_heads):
        if heads != heads_real:
            x = jnp.concatenate([x, jnp.zeros_like(x[:1])], axis=0)
        flat.append(x.reshape(rows, tokens))
    leaves = tokens // LEAF
    depth_local = leaves.bit_length() - 1
    depth_all = (leaves * seq_count).bit_length() - 1
    levels = list(range(1, depth_all))
    far_levels = [l for l in levels if l >= depth_local]
    coarse = lambda l: min(LEAF, tokens >> l)
    vm = pltpu.VMEM
    scratch = [
        vm(morton_order.shape, jnp.int32),
        pltpu.SMEM(leaf_counts.shape, jnp.int32),
        vm((3 * rows, tokens), BF),
        vm((2 * rows + PAD, tokens), BF),
        vm((tokens, 2 * rows), BF),
        vm((tokens + 2 * LEAF, rows), BF),
        vm((rows, tokens + 2 * LEAF), BF),
        vm((rows, tokens), F32),
        vm((2 * heads + (-2 * heads) % 8, tokens), F32),
    ]
    scratch += [vm((coarse(l), min(LEAF << l, tokens)), BF) for l in levels]
    near_blocks = sum(tokens // (LEAF << l) for l in levels if l not in far_levels)
    scratch += [
        vm((near_blocks, 2 * rows, LEAF), BF),
        vm((near_blocks, LEAF, 2 * rows), BF),
        vm((near_blocks, 2 * rows + PAD, LEAF), BF),
        vm((near_blocks, LEAF, rows), F32),
        vm((near_blocks, heads, 2 * (width + PAD) + PAD, LEAF), BF),
    ]
    scratch += [vm((heads, 2 * (width + PAD) + PAD, tokens >> l), BF) for l in far_levels]
    scratch += [vm((2 * rows, tokens >> l), BF) for l in far_levels]
    scratch += [vm((tokens >> l, rows), jnp.int16) for l in far_levels]
    scratch += [vm((rows + PAD, tokens >> l), jnp.int16) for l in far_levels]
    scratch += [vm((LEAF, rows), jnp.int16) for l in far_levels]
    scratch += [
        vm((1 << (l - depth_local), rows + PAD, tokens >> l), jnp.int16) for l in far_levels
    ]
    sem = pltpu.SemaphoreType.DMA
    scratch += [sem((5,)), sem((4,)), sem((4,))]
    scratch += [sem((2 << (l - depth_local),)) for l in far_levels] * 2
    out = pl.pallas_call(
        functools.partial(kernel, (heads, width, tokens, seq_count)),
        out_shape=jax.ShapeDtypeStruct((rows, tokens), BF),
        in_specs=[pl.BlockSpec(memory_space=pltpu.HBM)] * 5,
        out_specs=pl.BlockSpec(memory_space=pltpu.VMEM),
        scratch_shapes=scratch,
        compiler_params=pltpu.CompilerParams(
            collective_id=0, has_side_effects=True, vmem_limit_bytes=VMEM_LIMIT
        ),
    )(*flat, morton_order, leaf_counts)
    return out.reshape(heads, width, tokens)[:heads_real]


def solution(mesh):
    placed = (
        P("head", None, ("grp", "seq")),
        P("head", None, ("grp", "seq")),
        P("head", None, ("grp", "seq")),
        P(("grp", "seq"), None),
        P("grp"),
    )
    return jax.shard_map(
        shards,
        mesh=mesh,
        in_specs=placed,
        out_specs=P("head", None, ("grp", "seq")),
        check_vma=False,
    )
```

```python
import functools
import math

import jax
import jax.numpy as jnp
from jax import lax
from jax.experimental import pallas as pl
from jax.experimental.pallas import tpu as pltpu
from jax.sharding import PartitionSpec as P

LEAF = 256
NEG = -1e30
BF = jnp.bfloat16
F32 = jnp.float32
PAD = 16
BOUND = 10.0
STEPS = 32700.0
VMEM_LIMIT = 63 * 1024 * 1024 + 512 * 1024


def dot(a, b, dims=((1,), (0,))):
    return lax.dot_general(a, b, (dims, ((), ())), preferred_element_type=F32)


def split(x):
    hi = x.astype(BF)
    return hi, (x - hi.astype(F32)).astype(BF)


def kernel(cfg, *refs):
    heads, width, tokens, seq_count = cfg
    rows = heads * width
    leaves = tokens // LEAF
    depth_local = leaves.bit_length() - 1
    depth_all = (leaves * seq_count).bit_length() - 1
    levels = list(range(1, depth_all))
    far_levels = [l for l in levels if l >= depth_local]
    scale = math.log2(math.e) / math.sqrt(width)
    refs = list(refs)
    take = lambda n: [refs.pop(0) for _ in range(n)]
    q_hbm, k_hbm, v_hbm, order_hbm, counts_hbm, out = take(6)
    order, counts = take(2)
    xin, xp, kva, ktx, vx, num, stat = take(7)
    us = dict(zip(levels, take(len(levels))))
    qb, kmb, vvb, biasb, fb = take(5)
    fs = dict(zip(far_levels, take(len(far_levels))))
    qs = dict(zip(far_levels, take(len(far_levels))))
    kmp = dict(zip(far_levels, take(len(far_levels))))
    vvp = dict(zip(far_levels, take(len(far_levels))))
    kmr = dict(zip(far_levels, take(len(far_levels))))
    vvr = dict(zip(far_levels, take(len(far_levels))))
    in_sem, halo_send, halo_recv = take(3)
    far_send = dict(zip(far_levels, take(len(far_levels))))
    far_recv = dict(zip(far_levels, take(len(far_levels))))

    seq = lax.axis_index("seq")
    has_left, has_right = seq > 0, seq < seq_count - 1

    loads = [
        pltpu.make_async_copy(src, xin.at[pl.ds(i * rows, rows)], in_sem.at[i])
        for i, src in enumerate((q_hbm, k_hbm, v_hbm))
    ]
    loads.append(pltpu.make_async_copy(order_hbm, order, in_sem.at[3]))
    loads.append(pltpu.make_async_copy(counts_hbm, counts, in_sem.at[4]))
    for load in loads:
        load.start()
    barrier = pltpu.get_barrier_semaphore()
    for step in range(1, seq_count):
        other = lax.rem(seq + step, seq_count)
        pl.semaphore_signal(
            barrier, inc=1, device_id={"seq": other}, device_id_type=pl.DeviceIdType.MESH
        )

    @pl.when(jnp.logical_not(has_left))
    def _():
        ktx[0:LEAF, :] = jnp.zeros((LEAF, rows), BF)
        vx[:, 0:LEAF] = jnp.zeros((rows, LEAF), BF)

    @pl.when(jnp.logical_not(has_right))
    def _():
        ktx[tokens + LEAF :, :] = jnp.zeros((LEAF, rows), BF)
        vx[:, tokens + LEAF :] = jnp.zeros((rows, LEAF), BF)

    def count_of(n):
        leaf = seq * leaves + n
        total = leaves * seq_count
        inside = jnp.logical_and(leaf >= 0, leaf < total)
        return jnp.where(inside, counts[jnp.clip(leaf, 0, total - 1)], 0)

    def build(level):
        u = us[level]
        r = lax.broadcasted_iota(jnp.int32, u.shape, 0)
        t = lax.broadcasted_iota(jnp.int32, u.shape, 1)
        u[...] = jnp.where((t >> level) == r, 1.0, 0.0).astype(BF)

    for level in levels:
        build(level)
    for load in loads:
        load.wait()

    def permute(n):
        at = n * LEAF
        if not isinstance(n, int):
            at = pl.multiple_of(at, LEAF)
        picks = order[0:1, pl.ds(at, LEAF)]
        spots = lax.broadcasted_iota(jnp.int16, (tokens, LEAF), 0)
        wanted = jnp.broadcast_to(picks, (PAD, LEAF)).astype(jnp.int16)[0:1]
        hot = jnp.where(spots == wanted, jnp.ones((), BF), jnp.zeros((), BF))
        moved = dot(xin[...], hot)
        count = count_of(n)
        query, key, value = moved[:rows], moved[rows : 2 * rows], moved[2 * rows :]
        key_t = key.T
        on_row = lax.broadcasted_iota(jnp.int32, (rows, LEAF), 1) < count
        on_col = lax.broadcasted_iota(jnp.int32, (LEAF, rows), 0) < count
        xp[0:rows, pl.ds(at, LEAF)] = query.astype(BF)
        xp[rows : 2 * rows, pl.ds(at, LEAF)] = jnp.where(on_row, value, 0.0).astype(BF)
        xp[2 * rows :, pl.ds(at, LEAF)] = jnp.where(on_row[:PAD], 1.0, 0.0).astype(BF)
        kva[pl.ds(at, LEAF), 0:rows] = jnp.where(on_col, key_t, 0.0).astype(BF)
        kva[pl.ds(at, LEAF), rows:] = jnp.where(on_col, 1.0, 0.0).astype(BF)
        ktx[pl.ds(at + LEAF, LEAF), :] = key_t.astype(BF)
        vx[:, pl.ds(at + LEAF, LEAF)] = value.astype(BF)

    def remote(src, dst, send, recv, target):
        return pltpu.make_async_remote_copy(
            src_ref=src,
            dst_ref=dst,
            send_sem=send,
            recv_sem=recv,
            device_id={"seq": target},
            device_id_type=pl.DeviceIdType.MESH,
        )

    def halo(side):
        start, end = (LEAF, tokens + LEAF) if side == 0 else (tokens, 0)
        target = jnp.maximum(seq - 1, 0) if side == 0 else jnp.minimum(seq + 1, seq_count - 1)
        return (
            remote(
                ktx.at[pl.ds(start, LEAF)],
                ktx.at[pl.ds(end, LEAF)],
                halo_send.at[2 * side],
                halo_recv.at[2 * side],
                target,
            ),
            remote(
                vx.at[:, pl.ds(start, LEAF)],
                vx.at[:, pl.ds(end, LEAF)],
                halo_send.at[2 * side + 1],
                halo_recv.at[2 * side + 1],
                target,
            ),
        )

    @pl.loop(0, leaves)
    def _(i):
        n = jnp.where(i == 0, 0, jnp.where(i == 1, leaves - 1, i - 1))
        permute(n)

        @pl.when(i == 1)
        def _():
            pl.semaphore_wait(barrier, seq_count - 1)

        @pl.when(jnp.logical_and(i == 1, has_left))
        def _():
            for copy in halo(0):
                copy.start()

        @pl.when(jnp.logical_and(i == 1, has_right))
        def _():
            for copy in halo(1):
                copy.start()

    def pool(level, off, span):
        u = us[level][...]
        kk = dot(u, kva[pl.ds(off, span), :])
        mass = kk[:, rows:]
        mean = kk[:, :rows] / jnp.maximum(mass, 1.0)
        xx = dot(xp[:, pl.ds(off, span)], u, ((1,), (1,)))
        q_hi, q_lo = split(xx[:rows] * (1.0 / 2**level))
        return (q_hi, q_lo), mean, xx[rows : 2 * rows], xx[2 * rows :], mass

    def pack(mean, sums, masses):
        v_hi, v_lo = split(sums)
        km = jnp.concatenate(split(mean), axis=1)
        return km, jnp.concatenate([v_hi, v_lo, masses.astype(BF)], axis=0)

    def fixed(x, bound):
        return jnp.floor(x * (STEPS / bound) + 0.5).astype(jnp.int32).astype(jnp.int16)

    def unfixed(x, bound):
        return x.astype(jnp.int32).astype(F32) * (bound / STEPS)

    def only(x, head):
        blank = jnp.zeros((width, x.shape[1]), x.dtype)
        return jnp.concatenate(
            [x[h * width : (h + 1) * width] if h == head else blank for h in range(heads)],
            axis=0,
        )

    def far(query, km, vvs, bias, store):
        q_hi, q_lo = query
        count = q_hi.shape[1]
        for h in range(heads):
            hi, lo = only(q_hi, h), only(q_lo, h)
            s = dot(km, jnp.concatenate([hi, hi], axis=0)) + dot(km[:, :rows], lo)
            if count <= 128:
                s = s + bias[:, :count]
            else:
                s = s + jnp.concatenate([bias[:, :128]] * (count // 128), axis=1)
            best = jnp.max(s, axis=0, keepdims=True).astype(BF)
            w_hi, w_lo = split(jnp.exp2((s - best.astype(F32)) * scale))
            step = 0
            acc = jnp.zeros((width + PAD, count), F32)
            for vv in vvs:
                keys = vv.shape[1]
                v_hi = vv[h * width : (h + 1) * width]
                v_lo = vv[rows + h * width : rows + (h + 1) * width]
                mass = vv[2 * rows :]
                left = jnp.concatenate([v_hi, mass], axis=0)
                both = dot(jnp.concatenate([left, v_lo], axis=0), w_hi[step : step + keys])
                low = jnp.concatenate([both[width + PAD :], jnp.zeros((PAD, count), F32)], axis=0)
                acc = acc + both[: width + PAD] + low + dot(left, w_lo[step : step + keys])
                step += keys
            a_hi, a_lo = split(acc)
            tops = jnp.broadcast_to(best.astype(F32), (PAD, count)).astype(BF)
            store(h, jnp.concatenate([a_hi, a_lo, tops], axis=0))

    def far_copies(level):
        bit = level - depth_local
        nb = 1 << bit
        part = tokens >> level
        slot = lax.rem(seq, nb)
        base = ((seq >> bit) ^ 1) << bit
        copies = []
        for j in range(nb):
            target = base + j
            copies.append(
                remote(
                    kmp[level],
                    kmr[level].at[pl.ds(pl.multiple_of(slot * part, part), part)],
                    far_send[level].at[2 * j],
                    far_recv[level].at[2 * slot],
                    target,
                )
            )
            copies.append(
                remote(
                    vvp[level],
                    vvr[level].at[slot],
                    far_send[level].at[2 * j + 1],
                    far_recv[level].at[2 * slot + 1],
                    target,
                )
            )
        return copies

    for level in reversed(far_levels):
        (q_hi, q_lo), mean, sums, masses, _ = pool(level, 0, tokens)
        qs[level][0:rows, :] = q_hi
        qs[level][rows:, :] = q_lo
        kmp[level][...] = fixed(mean, BOUND)
        vvp[level][0:rows, :] = fixed(sums, BOUND * 2**level)
        vvp[level][rows:, :] = masses.astype(jnp.int32).astype(jnp.int16)
        for copy in far_copies(level):
            copy.start()

    first = 0
    for level in levels:
        if level in far_levels:
            continue
        span = LEAF << level
        blocks = tokens // span
        start = first

        @pl.loop(0, blocks)
        def _(i):
            (q_hi, q_lo), mean, sums, masses, mass = pool(
                level, pl.multiple_of(i * span, span), span
            )
            km, vv = pack(mean, sums, masses)
            qb[start + i, 0:rows, :] = q_hi
            qb[start + i, rows:, :] = q_lo
            kmb[start + i] = km
            vvb[start + i] = vv
            biasb[start + i] = jnp.where(mass > 0, 0.0, NEG)

        first += blocks

    @pl.loop(0, first, unroll=2)
    def _(i):
        query = (qb[i, 0:rows, :], qb[i, rows:, :])
        other = i + 1 - 2 * lax.rem(i, 2)

        def store(h, value):
            fb[i, h] = value

        far(query, kmb[other], [vvb[other]], biasb[other], store)

    def near(n):
        at = n * LEAF
        if not isinstance(n, int):
            at = pl.multiple_of(at, LEAF)
        window = ktx[pl.ds(at, 3 * LEAF), :]
        query = xp[0:rows, pl.ds(at, LEAF)]
        spots = lax.broadcasted_iota(jnp.int32, (LEAF, LEAF), 0)
        for h in range(heads):
            s = dot(window, only(query, h))
            s = jnp.concatenate(
                [
                    jnp.where(spots < count_of(n - 1 + i), s[i * LEAF : (i + 1) * LEAF], NEG)
                    for i in range(3)
                ],
                axis=0,
            )
            best = jnp.max(s, axis=0, keepdims=True)
            w = jnp.exp2((s - best) * scale)
            total = jnp.sum(w, axis=0, keepdims=True)
            value = vx[h * width : (h + 1) * width, pl.ds(at, 3 * LEAF)]
            num[h * width : (h + 1) * width, pl.ds(at, LEAF)] = dot(value, w.astype(BF))
            stat[2 * h : 2 * h + 1, pl.ds(at, LEAF)] = best
            stat[2 * h + 1 : 2 * h + 2, pl.ds(at, LEAF)] = total

    if leaves > 2:

        @pl.loop(1, leaves - 1, unroll=2)
        def _(n):
            near(n)

    @pl.when(has_right)
    def _():
        for copy in halo(0):
            copy.wait_recv()

    @pl.when(has_left)
    def _():
        for copy in halo(1):
            copy.wait_recv()

    @pl.loop(0, 2, unroll=2)
    def _(i):
        near(i * (leaves - 1))

    for level in far_levels:
        nb = 1 << (level - depth_local)
        part = tokens >> level
        for i in range(nb):
            remote(
                kmp[level], kmr[level].at[pl.ds(i * part, part)],
                far_send[level].at[2 * i], far_recv[level].at[2 * i], seq,
            ).wait_recv()
            remote(
                vvp[level], vvr[level].at[i],
                far_send[level].at[2 * i + 1], far_recv[level].at[2 * i + 1], seq,
            ).wait_recv()
        query = (qs[level][0:rows, :], qs[level][rows:, :])
        means = unfixed(kmr[level][...], BOUND)
        vvs = []
        for i in range(nb):
            sums = unfixed(vvr[level][i, 0:rows], BOUND * 2**level)
            masses = vvr[level][i, rows:].astype(jnp.int32).astype(F32)
            km, vv = pack(means, sums, masses)
            vvs.append(vv)
        ones = jnp.ones((PAD, 128), BF)
        mass = jnp.concatenate(
            [dot(vv[2 * rows :], ones, ((0,), (0,))) for vv in vvs], axis=0
        )
        bias = jnp.where(mass > 0, 0.0, NEG)

        def store(h, value):
            fs[level][h] = value

        far(query, km, vvs, bias, store)

    base_of, first = {}, 0
    for level in levels:
        base_of[level] = first
        first += tokens // (LEAF << level)

    def finish(n):
        at = pl.multiple_of(n * LEAF, LEAF)
        for h in range(heads):
            near_best = stat[2 * h : 2 * h + 1, pl.ds(at, LEAF)]
            near_total = stat[2 * h + 1 : 2 * h + 2, pl.ds(at, LEAF)]
            blocks = []
            best = near_best
            size = width + PAD
            for level in levels:
                if level in far_levels:
                    f = fs[level][h]
                    u = us[level][:, pl.ds(at, LEAF)]
                else:
                    g = 1 << level
                    f = fb[base_of[level] + (n >> level), h]
                    u = us[level][:, pl.ds(pl.multiple_of((n & (g - 1)) * LEAF, LEAF), LEAF)]
                up = dot(f, u)
                top = up[2 * size : 2 * size + 1]
                blocks.append((up[:size] + up[size : 2 * size], top))
                best = jnp.maximum(best, top)
            factor = jnp.exp2((near_best - best) * scale)
            top = num[h * width : (h + 1) * width, pl.ds(at, LEAF)] * factor
            bottom = near_total * factor
            for block, level_best in blocks:
                factor = jnp.exp2((level_best - best) * scale)
                top = top + block[:width] * factor
                bottom = bottom + block[width : width + 1] * factor
            out[h * width : (h + 1) * width, pl.ds(at, LEAF)] = (top * (1.0 / bottom)).astype(BF)

    @pl.loop(0, leaves, unroll=2)
    def _(n):
        finish(n)

    @pl.when(has_left)
    def _():
        for copy in halo(0):
            copy.wait_send()

    @pl.when(has_right)
    def _():
        for copy in halo(1):
            copy.wait_send()

    for level in far_levels:
        for copy in far_copies(level):
            copy.wait_send()


def shards(q_heads, k_heads, v_heads, morton_order, leaf_counts):
    heads_real, width, tokens = q_heads.shape
    heads = heads_real + heads_real % 2
    seq_count = lax.axis_size("seq")
    rows = heads * width
    flat = []
    for x in (q_heads, k_heads, v_heads):
        if heads != heads_real:
            x = jnp.concatenate([x, jnp.zeros_like(x[:1])], axis=0)
        flat.append(x.reshape(rows, tokens))
    leaves = tokens // LEAF
    depth_local = leaves.bit_length() - 1
    depth_all = (leaves * seq_count).bit_length() - 1
    levels = list(range(1, depth_all))
    far_levels = [l for l in levels if l >= depth_local]
    coarse = lambda l: min(LEAF, tokens >> l)
    vm = pltpu.VMEM
    scratch = [
        vm(morton_order.shape, jnp.int32),
        pltpu.SMEM(leaf_counts.shape, jnp.int32),
        vm((3 * rows, tokens), BF),
        vm((2 * rows + PAD, tokens), BF),
        vm((tokens, 2 * rows), BF),
        vm((tokens + 2 * LEAF, rows), BF),
        vm((rows, tokens + 2 * LEAF), BF),
        vm((rows, tokens), F32),
        vm((2 * heads + (-2 * heads) % 8, tokens), F32),
    ]
    scratch += [vm((coarse(l), min(LEAF << l, tokens)), BF) for l in levels]
    near_blocks = sum(tokens // (LEAF << l) for l in levels if l not in far_levels)
    scratch += [
        vm((near_blocks, 2 * rows, LEAF), BF),
        vm((near_blocks, LEAF, 2 * rows), BF),
        vm((near_blocks, 2 * rows + PAD, LEAF), BF),
        vm((near_blocks, LEAF, rows), F32),
        vm((near_blocks, heads, 2 * (width + PAD) + PAD, LEAF), BF),
    ]
    scratch += [vm((heads, 2 * (width + PAD) + PAD, tokens >> l), BF) for l in far_levels]
    scratch += [vm((2 * rows, tokens >> l), BF) for l in far_levels]
    scratch += [vm((tokens >> l, rows), jnp.int16) for l in far_levels]
    scratch += [vm((rows + PAD, tokens >> l), jnp.int16) for l in far_levels]
    scratch += [vm((LEAF, rows), jnp.int16) for l in far_levels]
    scratch += [
        vm((1 << (l - depth_local), rows + PAD, tokens >> l), jnp.int16) for l in far_levels
    ]
    sem = pltpu.SemaphoreType.DMA
    scratch += [sem((5,)), sem((4,)), sem((4,))]
    scratch += [sem((2 << (l - depth_local),)) for l in far_levels] * 2
    out = pl.pallas_call(
        functools.partial(kernel, (heads, width, tokens, seq_count)),
        out_shape=jax.ShapeDtypeStruct((rows, tokens), BF),
        in_specs=[pl.BlockSpec(memory_space=pltpu.HBM)] * 5,
        out_specs=pl.BlockSpec(memory_space=pltpu.VMEM),
        scratch_shapes=scratch,
        compiler_params=pltpu.CompilerParams(
            collective_id=0, has_side_effects=True, vmem_limit_bytes=VMEM_LIMIT
        ),
    )(*flat, morton_order, leaf_counts)
    return out.reshape(heads, width, tokens)[:heads_real]


def solution(mesh):
    placed = (
        P("head", None, ("grp", "seq")),
        P("head", None, ("grp", "seq")),
        P("head", None, ("grp", "seq")),
        P(("grp", "seq"), None),
        P("grp"),
    )
    return jax.shard_map(
        shards,
        mesh=mesh,
        in_specs=placed,
        out_specs=P("head", None, ("grp", "seq")),
        check_vma=False,
    )
```
